128 devices in a mesh: row: 16 (over y, x), col: 8 (over z, core).
Axes of the slice: x: 4, y: 4, z: 4, core: 2. Of those that a mesh axis runs over, the one named last changes fastest.
Arguments:
- matrix: float32 [16384, 16384], P('row', 'col'), as said below
Outputs:
- factored: float32 [16384, 16384], P('row', 'col')
Inputs may be any that keep to these rules, and one draw needn't show every extreme that they name: matrix, read as A by the first step, is symmetric and positive definite.
All inputs are finite; a program needn't handle non-finite values.
Results may differ from the reference program's by a relative error of at most 0.00028.
Values sent between devices are 32-bit elements; how exact they have to be, the bound alone decides.
No kernel may reach another device: no remote copies, remote signals or barrier semaphores. Data moves between devices by JAX's collectives and lax.ppermute only.
A program may use at most 128 MiB of HBM per device.

```python
import math
import jax
import jax.numpy as jnp
from jax import lax

TILE = 256
ORDER = 16384
TR_DEV = 4
TC_DEV = 8
N_ROW = 16
N_COL = 8


def matern_block(row_points, col_points, reach):
    diff_x = row_points[:, 0:1] - col_points[None, :, 0]
    diff_y = row_points[:, 1:2] - col_points[None, :, 1]
    diff_z = row_points[:, 2:3] - col_points[None, :, 2]
    dist = jnp.sqrt(diff_x * diff_x + diff_y * diff_y + diff_z * diff_z)
    scaled = math.sqrt(3.0) * dist / reach
    return (1.0 + scaled) * jnp.exp(-scaled)


def draw_matrix(key, part):
    key = jax.random.fold_in(key, 11)
    point_key = jax.random.fold_in(key, 0)
    nugget_key = jax.random.fold_in(key, 2)
    second_key = jax.random.fold_in(key, 3)
    points = jax.random.uniform(point_key, (ORDER, 3), jnp.float32)
    others = jax.random.uniform(second_key, (ORDER, 3), jnp.float32)
    nuggets = jax.random.uniform(nugget_key, (ORDER,), jnp.float32, 0.5, 1.5)
    stored = jnp.arange(ORDER, dtype=jnp.int32)
    row_map = (stored // TILE % TR_DEV * N_ROW + stored // (TR_DEV * TILE)) * TILE + stored % TILE
    col_map = (stored // TILE % TC_DEV * N_COL + stored // (TC_DEV * TILE)) * TILE + stored % TILE
    reach = 0.2
    first = matern_block(points[row_map], points[col_map], reach)
    same = jnp.where(row_map[:, None] == col_map[None, :], 1.0, 0.0)
    first = first + same * nuggets[row_map][:, None]
    second = matern_block(others[row_map], others[col_map], 0.6 * reach)
    second = second * 0.25
    return (first + second).astype(jnp.float32)


def setup_inputs(seed: int = 0) -> dict:
    key_of = jax.random.split(jax.random.key(seed), 2)
    return {
        "matrix": draw_matrix(jax.random.fold_in(key_of[1], 71), 0),
    }


def to_global(stored):
    shaped = stored.reshape(N_ROW, TR_DEV, TILE, N_COL, TC_DEV, TILE)
    return shaped.transpose(1, 0, 2, 4, 3, 5).reshape(ORDER, ORDER)

def to_stored(whole):
    shaped = whole.reshape(TR_DEV, N_ROW, TILE, TC_DEV, N_COL, TILE)
    return shaped.transpose(1, 0, 2, 4, 3, 5).reshape(ORDER, ORDER)

def reference(matrix):
    current = to_global(matrix)
    for panel_index in range(2):
        start = panel_index * TILE
        below = start + TILE
        factor = jnp.linalg.cholesky(current[start:below, start:below])
        solved = jax.scipy.linalg.solve_triangular(factor, current[below:, start:below].T, lower=True).T
        update = jnp.dot(solved.astype(jnp.float32), solved.T.astype(jnp.float32), precision=lax.Precision.HIGHEST, preferred_element_type=jnp.float32)
        current = current.at[below:, below:].set(current[below:, below:] - update)
        current = current.at[start:below, start:below].set(factor)
        current = current.at[below:, start:below].set(solved)
        current = current.at[:start, start:below].set(jnp.zeros((start, TILE), jnp.float32))
        current = current.at[start:below, below:].set(jnp.zeros((TILE, ORDER - below), jnp.float32))
    return to_stored(current)
```

```python
import jax
import jax.numpy as jnp
from jax import lax
from jax.experimental import pallas as pl
from jax.experimental.pallas import tpu as pltpu
from jax.sharding import PartitionSpec as P

TILE = 256
BLOCK = 128
F32 = jnp.float32
BF16 = jnp.bfloat16
HIGHEST = lax.Precision.HIGHEST


def device_id(y, x, z, c):
    return ((4 * y + x) * 4 + z) * 2 + c


def pairs(moves):
    return [(device_id(*a), device_id(*b)) for a, b in moves]


R4 = range(4)
R2 = range(2)


def send(value, moves):
    return lax.ppermute(value, ("row", "col"), pairs(moves))


def split3(x):
    hi = x.astype(BF16).astype(F32)
    rest = x - hi
    mid = rest.astype(BF16).astype(F32)
    return hi, mid, rest - mid


def stacked(x, left):
    hi, mid, lo = split3(x)
    parts = [hi, hi, mid, hi, lo, mid] if left else [hi, mid, hi, lo, hi, mid]
    return jnp.concatenate(parts, axis=0).astype(BF16)


def dot_tn(a, b, precision=None):
    return lax.dot_general(
        a, b, (((0,), (0,)), ((), ())), precision=precision, preferred_element_type=F32
    )


def spread(x):
    return jnp.broadcast_to(x, (8, BLOCK))


def factor_block(rows):
    groups = BLOCK // 8
    sub = lax.broadcasted_iota(jnp.int32, (8, BLOCK), 0)
    lane = lax.broadcasted_iota(jnp.int32, (8, BLOCK), 1)
    a = list(rows)
    w = [jnp.where(lane == sub + 8 * g, 1.0, 0.0).astype(F32) for g in range(groups)]
    upper, inverse = [], []
    for g in range(groups):
        r, v = a[g], w[g]
        cols = [spread(r[:, 8 * g + i : 8 * g + i + 1]) for i in range(8)]
        pivots = None
        for i in range(8):
            p = spread(cols[i][i : i + 1, :])
            pivots = p if pivots is None else jnp.where(sub == i, p, pivots)
            if i == 7:
                break
            m = jnp.where(sub > i, cols[i] / p, 0.0)
            r = r - m * spread(r[i : i + 1, :])
            v = v - m * spread(v[i : i + 1, :])
            for j in range(i + 1, 8):
                cols[j] = cols[j] - m * spread(cols[j][i : i + 1, :])
        s = lax.rsqrt(pivots)
        s = s * (1.5 - 0.5 * pivots * s * s)
        r = jnp.where(lane >= sub + 8 * g, r * s, 0.0)
        v = v * s
        upper.append(r)
        inverse.append(v)
        if g < groups - 1:
            t = dot_tn(stacked(r, True), stacked(jnp.concatenate([r, v], axis=1), False))
            for h in range(g + 1, groups):
                a[h] = a[h] - t[8 * h : 8 * h + 8, :BLOCK]
                w[h] = w[h] - t[8 * h : 8 * h + 8, BLOCK:]
    return jnp.concatenate(upper, axis=0), jnp.concatenate(inverse, axis=0)


def factor_kernel(d00, d10, d11, v_ref, l00, l11, m):
    n, b = 2 * TILE, BLOCK
    count = n // b
    m[0:TILE, 0:TILE] = d00[...]
    m[0:TILE, TILE:n] = d10[...].T
    m[TILE:n, TILE:n] = d11[...]
    v_ref[...] = jnp.zeros((n, n), F32)
    for k in range(count):
        o = k * b
        e = o + b
        uk, vk = factor_block([m[o + 8 * g : o + 8 * g + 8, o:e] for g in range(b // 8)])
        m[o:e, o:e] = uk
        if k > 0:
            v_ref[o:e, 0:o] = jnp.dot(
                vk, v_ref[o:e, 0:o], precision=HIGHEST, preferred_element_type=F32
            )
        v_ref[o:e, o:e] = vk
        if k < count - 1:
            row = jnp.dot(vk, m[o:e, e:n], precision=HIGHEST, preferred_element_type=F32)
            m[o:e, e:n] = row
            for j in range(k + 1, count):
                s = j * b
                t = s + b
                left = row[:, s - e : t - e]
                m[s:t, s:n] = m[s:t, s:n] - dot_tn(left, row[:, s - e :], HIGHEST)
                v_ref[s:t, 0:e] = v_ref[s:t, 0:e] - dot_tn(left, v_ref[o:e, 0:e], HIGHEST)
    r = lax.broadcasted_iota(jnp.int32, (TILE, TILE), 0)
    c = lax.broadcasted_iota(jnp.int32, (TILE, TILE), 1)
    l00[...] = jnp.where(r >= c, m[0:TILE, 0:TILE].T, 0.0)
    l11[...] = jnp.where(r >= c, m[TILE:n, TILE:n].T, 0.0)


def factor(d00, d10, d11):
    n = 2 * TILE
    vmem = pl.BlockSpec(memory_space=pltpu.VMEM)
    return pl.pallas_call(
        factor_kernel,
        out_shape=[
            jax.ShapeDtypeStruct((n, n), F32),
            jax.ShapeDtypeStruct((TILE, TILE), F32),
            jax.ShapeDtypeStruct((TILE, TILE), F32),
        ],
        in_specs=[vmem] * 3,
        out_specs=[vmem] * 3,
        scratch_shapes=[pltpu.VMEM((n, n), F32)],
        compiler_params=pltpu.CompilerParams(vmem_limit_bytes=16 * 2**20),
        cost_estimate=pl.CostEstimate(
            flops=15 * 10**9, bytes_accessed=3 * 2**20, transcendentals=0
        ),
    )(d00, d10, d11)


def halves(x):
    hi = x.astype(BF16)
    return hi, (x - hi.astype(F32)).astype(BF16)


def dot3(a, b, dims):
    ah, al = a
    bh, bl = b
    d = (dims, ((), ()))
    out = lax.dot_general(ah, bh, d, preferred_element_type=F32)
    out = out + lax.dot_general(ah, bl, d, preferred_element_type=F32)
    return out + lax.dot_general(al, bh, d, preferred_element_type=F32)


NT = ((1,), (1,))
NN = ((1,), (0,))
CHUNK = 512


def update_kernel(
    place, mat, v_hbm, l00, l11, mine_a, mine_b, other_a, other_b,
    x0, x1, x2, x3, y0, y1, y2, y3, out,
    m, o, ap, dq, v, lp, lph, lpl, lqh, lql, in_sem, piece_sem, out_sem,
):
    row, col = place[0], place[1]
    y, x = row // 4, row % 4
    c = col % 2
    rows, cols = mat.shape
    chunks = cols // CHUNK
    copies = []

    def fetch(src, dst):
        copy = pltpu.make_async_copy(src, dst, piece_sem.at[len(copies)])
        copy.start()
        copies.append(copy)

    half = rows // 2
    fetch(v_hbm, v)
    for ref, which, at in ((mine_a, c, 0), (mine_b, c, half), (other_a, 1 - c, 0), (other_b, 1 - c, half)):
        fetch(ref, ap.at[which, pl.ds(at, half), :])
    for k, ref in enumerate((x0, x1, x2, x3)):
        source = lax.rem(x + 4 - k, 4)
        second = jnp.logical_or(source == 1, source == 2).astype(jnp.int32)
        start = pl.multiple_of((source // 2) * 512, 512)
        fetch(ref, dq.at[second, :, pl.ds(start, 512)])
    for k, ref in enumerate((y0, y1, y2, y3)):
        source = lax.rem(y + 4 - k, 4)
        start = pl.multiple_of(1024 + source * 256, 256)
        fetch(ref, dq.at[:, :, pl.ds(start, 256)])
    loads = []
    for j in range(chunks):
        copy = pltpu.make_async_copy(
            mat.at[:, pl.ds(j * CHUNK, CHUNK)], m.at[:, pl.ds(j * CHUNK, CHUNK)], in_sem.at[j]
        )
        copy.start()
        loads.append(copy)

    for copy in copies[:5]:
        copy.wait()
    v00 = halves(v[0:TILE, 0:TILE])
    v10 = halves(v[TILE:, 0:TILE])
    v11 = halves(v[TILE:, TILE:])
    for i in range(rows // TILE):
        at = pl.ds(i * TILE, TILE)
        a0 = halves(ap[0, at, :])
        a1 = halves(ap[1, at, :])
        first = dot3(a0, v00, NT)
        second = dot3(a0, v10, NT) + dot3(a1, v11, NT)
        lp[at, 0:TILE] = first
        lp[at, TILE:] = second
        lph[at, 0:TILE], lpl[at, 0:TILE] = halves(first)
        lph[at, TILE:], lpl[at, TILE:] = halves(second)
    for copy in copies[5:]:
        copy.wait()
    stores = []
    for j in range(chunks):
        at = pl.ds(j * CHUNK, CHUNK)
        d0 = halves(dq[0, :, at])
        d1 = halves(dq[1, :, at])
        lqh[0:TILE, :], lql[0:TILE, :] = halves(dot3(v00, d0, NN))
        lqh[TILE:, :], lql[TILE:, :] = halves(dot3(v10, d0, NN) + dot3(v11, d1, NN))
        loads[j].wait()
        for i in range(rows // TILE):
            r = pl.ds(i * TILE, TILE)
            o[r, at] = m[r, at] - dot3(
                (lph[r, :], lpl[r, :]), (lqh[...], lql[...]), NN
            )

        @pl.when(row < 2)
        def _():
            o[0:TILE, at] = jnp.zeros((TILE, CHUNK), F32)

        if j == 0:
            @pl.when(col == 0)
            def _():
                o[:, 0:TILE] = lp[:, 0:TILE]

                @pl.when(row == 0)
                def _():
                    o[0:TILE, 0:TILE] = l00[...]

            @pl.when(col == 1)
            def _():
                o[:, 0:TILE] = lp[:, TILE:]

                @pl.when(row == 0)
                def _():
                    o[0:TILE, 0:TILE] = jnp.zeros((TILE, TILE), F32)

                @pl.when(row == 1)
                def _():
                    o[0:TILE, 0:TILE] = l11[...]

        copy = pltpu.make_async_copy(o.at[:, at], out.at[:, at], out_sem.at[j])
        copy.start()
        stores.append(copy)
    for copy in stores:
        copy.wait()


def update(place, mat, v, l00, l11, mine, other, xs, ys):
    rows, cols = mat.shape
    n = 2 * TILE
    chunks = cols // CHUNK
    hbm = pl.BlockSpec(memory_space=pl.ANY)
    vmem = pl.BlockSpec(memory_space=pltpu.VMEM)
    smem = pl.BlockSpec(memory_space=pltpu.SMEM)
    return pl.pallas_call(
        update_kernel,
        out_shape=jax.ShapeDtypeStruct((rows, cols), F32),
        in_specs=[smem, hbm, hbm, vmem, vmem] + [hbm] * 12,
        out_specs=hbm,
        scratch_shapes=[
            pltpu.VMEM((rows, cols), F32),
            pltpu.VMEM((rows, cols), F32),
            pltpu.VMEM((2, rows, TILE), F32),
            pltpu.VMEM((2, TILE, cols), F32),
            pltpu.VMEM((n, n), F32),
            pltpu.VMEM((rows, n), F32),
            pltpu.VMEM((rows, n), BF16),
            pltpu.VMEM((rows, n), BF16),
            pltpu.VMEM((n, CHUNK), BF16),
            pltpu.VMEM((n, CHUNK), BF16),
            pltpu.SemaphoreType.DMA((chunks,)),
            pltpu.SemaphoreType.DMA((13,)),
            pltpu.SemaphoreType.DMA((chunks,)),
        ],
        compiler_params=pltpu.CompilerParams(vmem_limit_bytes=48 * 2**20),
        cost_estimate=pl.CostEstimate(
            flops=10 * 10**9, bytes_accessed=24 * 2**20, transcendentals=0
        ),
    )(place, mat, v, l00, l11, *mine, *other, *xs, *ys)


def along(axis, table, cores=R2, fixed=None):
    fixed = fixed or {}
    names = "yxzc"
    ranges = [fixed.get(k, R4 if k != "c" else cores) for k in names]
    moves = []
    at = names.index(axis)
    for a, b in table:
        spans = list(ranges)
        spans[at] = (a,)
        for y in spans[0]:
            for x in spans[1]:
                for z in spans[2]:
                    for c in spans[3]:
                        src = [y, x, z, c]
                        dst = list(src)
                        dst[at] = b
                        moves.append((tuple(src), tuple(dst)))
    return moves


def spread_chain(value, core, order, root):
    fixed = {k: (root[k],) for k in "yxz"}
    for axis in order:
        s = root[axis]
        near, far, opposite = (s + 1) % 4, (s + 3) % 4, (s + 2) % 4
        first = send(value, along(axis, [(s, near)], (core,), fixed))
        value = value + first
        second = send(value, along(axis, [(s, far), (near, opposite)], (core,), fixed))
        value = value + second
        fixed[axis] = R4
    return value


def swap_cores(value):
    return send(value, [((y, x, z, c), (y, x, z, 1 - c)) for y in R4 for x in R4 for z in R4 for c in R2])


def shards(matrix):
    row = lax.axis_index("row")
    col = lax.axis_index("col")
    y, x = row // 4, row % 4
    z, c = col // 2, col % 2
    tile = matrix[0:TILE, 0:TILE]

    at_first = (row == 0) & (col == 0)
    at_second = (row == 1) & (col == 1)
    t00 = spread_chain(jnp.where(at_first, tile, 0.0), 0, "xyz", {"y": 0, "x": 0, "z": 0})
    t10 = send(tile, [((0, 1, 0, 0), (0, 1, 0, 1))])
    pair = jnp.where(at_second, jnp.stack([t10, tile]), 0.0)
    pair = spread_chain(pair, 1, "zyx", {"y": 0, "x": 1, "z": 0})
    t00 = t00 + send(t00, [((a, b, d, 0), (a, b, d, 1)) for a in R4 for b in R4 for d in R4])
    pair = pair + send(pair, [((a, b, d, 1), (a, b, d, 0)) for a in R4 for b in R4 for d in R4])
    v, l00, l11 = factor(t00, pair[0], pair[1])

    strip = matrix[:, 0:TILE]
    half = strip.shape[0] // 2
    own_a, own_b = strip[:half], strip[half:]
    at_zero = z == 0
    a1 = send(own_a, along("z", [(0, 1)]))
    b1 = send(own_b, along("z", [(0, 3)]))
    a2 = send(jnp.where(at_zero, own_a, a1), along("z", [(0, 3), (1, 2)]))
    b2 = send(jnp.where(at_zero, own_b, b1), along("z", [(0, 1), (3, 2)]))
    mine_a = jnp.where(at_zero, own_a, a1 + a2)
    mine_b = jnp.where(at_zero, own_b, b1 + b2)
    other_a = swap_cores(mine_a)
    other_b = swap_cores(mine_b)

    near = matrix[0:TILE, 0:512]
    far = matrix[0:TILE, 512:1024]
    moved = send(far, along("x", [(0, 3), (1, 2)], fixed={"y": (0,)}))
    quarter = jnp.where(x < 2, near, moved)
    top = y == 0
    qa, qb = quarter[:, :256], quarter[:, 256:]
    qa1 = send(qa, along("y", [(0, 1)]))
    qb1 = send(qb, along("y", [(0, 3)]))
    qa2 = send(jnp.where(top, qa, qa1), along("y", [(0, 3), (1, 2)]))
    qb2 = send(jnp.where(top, qb, qb1), along("y", [(0, 1), (3, 2)]))
    quarter = jnp.where(top, quarter, jnp.concatenate([qa1 + qa2, qb1 + qb2], axis=1))
    xs = [quarter] + [send(quarter, along("x", [(i, (i + k) % 4) for i in R4])) for k in (1, 2, 3)]

    parts = [matrix[0:TILE, 1024 + 256 * i : 1280 + 256 * i] for i in R4]
    got = [send(parts[k], along("y", [(0, k)], fixed={"x": (0, 1)})) for k in (1, 2, 3)]
    base = jnp.where(top, parts[0], got[0] + got[1] + got[2])
    e1 = send(base, along("x", [(0, 1), (1, 0)]))
    e2 = send(base, along("x", [(0, 3), (1, 2)]))
    e3 = send(e2, along("x", [(3, 2), (2, 3)]))
    kept = jnp.where(x < 2, base, e2)
    came = e1 + e3
    first_mine = (x == 0) | (x == 3)
    both = jnp.stack([jnp.where(first_mine, kept, came), jnp.where(first_mine, came, kept)])
    ys = [both] + [send(both, along("y", [(i, (i + k) % 4) for i in R4])) for k in (1, 2, 3)]

    place = jnp.stack([row, col]).astype(jnp.int32)
    return update(place, matrix, v, l00, l11, (mine_a, mine_b), (other_a, other_b), xs, ys)


def solution(mesh):
    return jax.shard_map(
        shards,
        mesh=mesh,
        in_specs=(P("row", "col"),),
        out_specs=P("row", "col"),
        check_vma=False,
    )
```

```python
import jax
import jax.numpy as jnp
from jax import lax
from jax.experimental import pallas as pl
from jax.experimental.pallas import tpu as pltpu
from jax.sharding import PartitionSpec as P

TILE = 256
BLOCK = 128
F32 = jnp.float32
BF16 = jnp.bfloat16
HIGHEST = lax.Precision.HIGHEST


def device_id(y, x, z, c):
    return ((4 * y + x) * 4 + z) * 2 + c


def pairs(moves):
    return [(device_id(*a), device_id(*b)) for a, b in moves]


R4 = range(4)
R2 = range(2)


def send(value, moves):
    return lax.ppermute(value, ("row", "col"), pairs(moves))


def split3(x):
    hi = x.astype(BF16).astype(F32)
    rest = x - hi
    mid = rest.astype(BF16).astype(F32)
    return hi, mid, rest - mid


def stacked(x, left):
    hi, mid, lo = split3(x)
    parts = [hi, hi, mid, hi, lo, mid] if left else [hi, mid, hi, lo, hi, mid]
    return jnp.concatenate(parts, axis=0).astype(BF16)


def dot_tn(a, b, precision=None):
    return lax.dot_general(
        a, b, (((0,), (0,)), ((), ())), precision=precision, preferred_element_type=F32
    )


def spread(x):
    return jnp.broadcast_to(x, (8, BLOCK))


def factor_block(rows):
    groups = BLOCK // 8
    sub = lax.broadcasted_iota(jnp.int32, (8, BLOCK), 0)
    lane = lax.broadcasted_iota(jnp.int32, (8, BLOCK), 1)
    a = list(rows)
    w = [jnp.where(lane == sub + 8 * g, 1.0, 0.0).astype(F32) for g in range(groups)]
    upper, inverse = [], []
    for g in range(groups):
        r, v = a[g], w[g]
        cols = [spread(r[:, 8 * g + i : 8 * g + i + 1]) for i in range(8)]
        pivots = None
        for i in range(8):
            p = spread(cols[i][i : i + 1, :])
            pivots = p if pivots is None else jnp.where(sub == i, p, pivots)
            if i == 7:
                break
            m = jnp.where(sub > i, cols[i] / p, 0.0)
            r = r - m * spread(r[i : i + 1, :])
            v = v - m * spread(v[i : i + 1, :])
            for j in range(i + 1, 8):
                cols[j] = cols[j] - m * spread(cols[j][i : i + 1, :])
        s = lax.rsqrt(pivots)
        s = s * (1.5 - 0.5 * pivots * s * s)
        r = jnp.where(lane >= sub + 8 * g, r * s, 0.0)
        v = v * s
        upper.append(r)
        inverse.append(v)
        if g < groups - 1:
            t = dot_tn(stacked(r, True), stacked(jnp.concatenate([r, v], axis=1), False))
            for h in range(g + 1, groups):
                a[h] = a[h] - t[8 * h : 8 * h + 8, :BLOCK]
                w[h] = w[h] - t[8 * h : 8 * h + 8, BLOCK:]
    return jnp.concatenate(upper, axis=0), jnp.concatenate(inverse, axis=0)


def factor_tile(m, v_ref, l_ref):
    b = BLOCK
    u0, v0 = factor_block([m[8 * g : 8 * g + 8, 0:b] for g in range(b // 8)])
    u01 = jnp.dot(v0, m[0:b, b:], precision=HIGHEST, preferred_element_type=F32)
    m[b:, b:] = m[b:, b:] - dot_tn(u01, u01, HIGHEST)
    u1, v1 = factor_block([m[b + 8 * g : b + 8 * g + 8, b:] for g in range(b // 8)])
    w = dot_tn(u01, v0, HIGHEST)
    zeros = jnp.zeros((b, b), F32)
    v_ref[0:b, 0:b] = v0
    v_ref[0:b, b:] = zeros
    v_ref[b:, 0:b] = -jnp.dot(v1, w, precision=HIGHEST, preferred_element_type=F32)
    v_ref[b:, b:] = v1
    l_ref[0:b, 0:b] = u0.T
    l_ref[0:b, b:] = zeros
    l_ref[b:, 0:b] = u01.T
    l_ref[b:, b:] = u1.T


def first_kernel(d00, v00, l00, m):
    m[...] = d00[...]
    factor_tile(m, v00, l00)


def second_kernel(d10, d11, v00, v10, v11, l11, m):
    u01 = lax.dot_general(
        v00[...], d10[...], (((1,), (1,)), ((), ())), precision=HIGHEST, preferred_element_type=F32
    )
    m[...] = d11[...] - dot_tn(u01, u01, HIGHEST)
    factor_tile(m, v11, l11)
    w = dot_tn(u01, v00[...], HIGHEST)
    v10[...] = -jnp.dot(v11[...], w, precision=HIGHEST, preferred_element_type=F32)


def factor_call(kernel, outs, *args):
    vmem = pl.BlockSpec(memory_space=pltpu.VMEM)
    return pl.pallas_call(
        kernel,
        out_shape=[jax.ShapeDtypeStruct((TILE, TILE), F32)] * outs,
        in_specs=[vmem] * len(args),
        out_specs=[vmem] * outs,
        scratch_shapes=[pltpu.VMEM((TILE, TILE), F32)],
        compiler_params=pltpu.CompilerParams(vmem_limit_bytes=16 * 2**20),
        cost_estimate=pl.CostEstimate(
            flops=10 * 10**9, bytes_accessed=2**20, transcendentals=0
        ),
    )(*args)


def halves(x):
    hi = x.astype(BF16)
    return hi, (x - hi.astype(F32)).astype(BF16)


def dot3(a, b, dims):
    ah, al = a
    bh, bl = b
    d = (dims, ((), ()))
    out = lax.dot_general(ah, bh, d, preferred_element_type=F32)
    out = out + lax.dot_general(ah, bl, d, preferred_element_type=F32)
    return out + lax.dot_general(al, bh, d, preferred_element_type=F32)


NT = ((1,), (1,))
NN = ((1,), (0,))
CHUNK = 512


def update_kernel(
    place, mat, v00_ref, v10_ref, v11_ref, l00, l11, mine, other, g0, g1, g2, g3, out,
    m, o, ap, dq, lp, lph, lpl, lqh, lql, in_sem, piece_sem, out_sem,
):
    row, col = place[0], place[1]
    y, x = row // 4, row % 4
    c = col % 2
    rows, cols = mat.shape
    chunks = cols // CHUNK
    copies = []

    def fetch(src, dst):
        copy = pltpu.make_async_copy(src, dst, piece_sem.at[len(copies)])
        copy.start()
        copies.append(copy)

    fetch(mine, ap.at[c])
    fetch(other, ap.at[1 - c])
    major = jnp.where(c == 0, x, y)
    for k, ref in enumerate((g0, g1, g2, g3)):
        source = lax.rem(major + 4 - k, 4)
        middle = jnp.logical_or(source == 1, source == 2).astype(jnp.int32)
        for j in range(2):
            panel = jnp.where(c == 0, middle, j)
            start = jnp.where(c == 0, (source // 2) * 1024 + 512 * j, source * 512)
            fetch(ref.at[j], dq.at[panel, :, pl.ds(pl.multiple_of(start, 512), 512)])
    loads = []
    for j in range(chunks):
        copy = pltpu.make_async_copy(
            mat.at[:, pl.ds(j * CHUNK, CHUNK)], m.at[:, pl.ds(j * CHUNK, CHUNK)], in_sem.at[j]
        )
        copy.start()
        loads.append(copy)

    for copy in copies[:2]:
        copy.wait()
    v00 = halves(v00_ref[...])
    v10 = halves(v10_ref[...])
    v11 = halves(v11_ref[...])
    for i in range(rows // TILE):
        at = pl.ds(i * TILE, TILE)
        a0 = halves(ap[0, at, :])
        a1 = halves(ap[1, at, :])
        first = dot3(a0, v00, NT)
        second = dot3(a0, v10, NT) + dot3(a1, v11, NT)
        lp[at, 0:TILE] = first
        lp[at, TILE:] = second
        lph[at, 0:TILE], lpl[at, 0:TILE] = halves(first)
        lph[at, TILE:], lpl[at, TILE:] = halves(second)
    for copy in copies[2:]:
        copy.wait()
    stores = []
    for j in range(chunks):
        at = pl.ds(j * CHUNK, CHUNK)
        d0 = halves(dq[0, :, at])
        d1 = halves(dq[1, :, at])
        lqh[0:TILE, :], lql[0:TILE, :] = halves(dot3(v00, d0, NN))
        lqh[TILE:, :], lql[TILE:, :] = halves(dot3(v10, d0, NN) + dot3(v11, d1, NN))
        loads[j].wait()
        for i in range(rows // TILE):
            r = pl.ds(i * TILE, TILE)
            o[r, at] = m[r, at] - dot3(
                (lph[r, :], lpl[r, :]), (lqh[...], lql[...]), NN
            )

        @pl.when(row < 2)
        def _():
            o[0:TILE, at] = jnp.zeros((TILE, CHUNK), F32)

        if j == 0:
            @pl.when(col == 0)
            def _():
                o[:, 0:TILE] = lp[:, 0:TILE]

                @pl.when(row == 0)
                def _():
                    o[0:TILE, 0:TILE] = l00[...]

            @pl.when(col == 1)
            def _():
                o[:, 0:TILE] = lp[:, TILE:]

                @pl.when(row == 0)
                def _():
                    o[0:TILE, 0:TILE] = jnp.zeros((TILE, TILE), F32)

                @pl.when(row == 1)
                def _():
                    o[0:TILE, 0:TILE] = l11[...]

        copy = pltpu.make_async_copy(o.at[:, at], out.at[:, at], out_sem.at[j])
        copy.start()
        stores.append(copy)
    for copy in stores:
        copy.wait()


def update(place, mat, v00, v10, v11, l00, l11, mine, other, pieces):
    rows, cols = mat.shape
    n = 2 * TILE
    chunks = cols // CHUNK
    hbm = pl.BlockSpec(memory_space=pl.ANY)
    vmem = pl.BlockSpec(memory_space=pltpu.VMEM)
    smem = pl.BlockSpec(memory_space=pltpu.SMEM)
    return pl.pallas_call(
        update_kernel,
        out_shape=jax.ShapeDtypeStruct((rows, cols), F32),
        in_specs=[smem, hbm] + [vmem] * 5 + [hbm] * 6,
        out_specs=hbm,
        scratch_shapes=[
            pltpu.VMEM((rows, cols), F32),
            pltpu.VMEM((rows, cols), F32),
            pltpu.VMEM((2, rows, TILE), F32),
            pltpu.VMEM((2, TILE, cols), F32),
            pltpu.VMEM((rows, n), F32),
            pltpu.VMEM((rows, n), BF16),
            pltpu.VMEM((rows, n), BF16),
            pltpu.VMEM((n, CHUNK), BF16),
            pltpu.VMEM((n, CHUNK), BF16),
            pltpu.SemaphoreType.DMA((chunks,)),
            pltpu.SemaphoreType.DMA((10,)),
            pltpu.SemaphoreType.DMA((chunks,)),
        ],
        compiler_params=pltpu.CompilerParams(vmem_limit_bytes=48 * 2**20),
        cost_estimate=pl.CostEstimate(
            flops=10 * 10**9, bytes_accessed=24 * 2**20, transcendentals=0
        ),
    )(place, mat, v00, v10, v11, l00, l11, mine, other, *pieces)


def along(axis, table, core, fixed=None):
    fixed = fixed or {}
    moves = []
    spans = [fixed.get(k, R4) for k in "yxz"]
    at = "yxz".index(axis)
    for a, b in table:
        spans[at] = (a,)
        for y in spans[0]:
            for x in spans[1]:
                for z in spans[2]:
                    dst = [y, x, z, core]
                    dst[at] = b
                    moves.append(((y, x, z, core), tuple(dst)))
    return moves


def swap_cores(value):
    return send(value, [((y, x, z, c), (y, x, z, 1 - c)) for y in R4 for x in R4 for z in R4 for c in R2])


def chain(value, place, root, orders, turns):
    c = place["c"]
    fixed = [{k: (root[k],) for k in "yxz"} for _ in R2]
    for step in range(3):
        axes = [orders[core][step] for core in R2]
        spots = []
        for core in R2:
            s, t = root[axes[core]], turns[core]
            spots.append((s, (s + t) % 4, (s - t) % 4, (s + 2) % 4))
        here = jnp.where(c == 0, place[axes[0]], place[axes[1]])

        def at(k):
            return here == jnp.where(c == 0, spots[0][k], spots[1][k])

        moves = []
        for core in R2:
            s, near, far, opposite = spots[core]
            moves += along(axes[core], [(s, near)], core, fixed[core])
        value = jnp.where(at(1), send(value, moves), value)
        moves = []
        for core in R2:
            s, near, far, opposite = spots[core]
            moves += along(axes[core], [(s, far), (near, opposite)], core, fixed[core])
        value = jnp.where(at(2) | at(3), send(value, moves), value)
        for core in R2:
            fixed[core][axes[core]] = R4
    return value


def shards(matrix):
    row = lax.axis_index("row")
    col = lax.axis_index("col")
    y, x = row // 4, row % 4
    z, c = col // 2, col % 2
    place = {"y": y, "x": x, "z": z, "c": c}
    zero_core = c == 0
    half = TILE // 2

    tile = matrix[0:TILE, 0:TILE]
    lower = send(tile[half:], [((0, 0, 0, 0), (0, 0, 0, 1))])
    part = jnp.where(zero_core, tile[:half], lower)
    part = chain(part, place, {"y": 0, "x": 0, "z": 0}, ("xyz", "yzx"), (1, 1))
    rest = swap_cores(part)
    d00 = jnp.concatenate([jnp.where(zero_core, part, rest), jnp.where(zero_core, rest, part)], axis=0)
    next_part = chain(tile, place, {"y": 0, "x": 1, "z": 0}, ("zxy", "zyx"), (1, -1))
    next_rest = swap_cores(next_part)
    d10 = jnp.where(zero_core, next_part, next_rest)
    d11 = jnp.where(zero_core, next_rest, next_part)

    v00, l00 = factor_call(first_kernel, 2, d00)
    v10, v11, l11 = factor_call(second_kernel, 3, d10, d11, v00)

    strip = matrix[:, 0:TILE]
    r1 = send(strip, along("z", [(0, 1)], 0) + along("z", [(0, 3)], 1))
    first_stop = jnp.where(zero_core, 1, 3)
    mine = jnp.where(z == first_stop, r1, strip)
    r2 = send(mine, along("z", [(0, 3), (1, 2)], 0) + along("z", [(0, 1), (3, 2)], 1))
    mine = jnp.where((z == 0) | (z == first_stop), mine, r2)
    other = swap_cores(mine)

    pick = lambda a, b: jnp.where(zero_core, a, b)
    quarters = [matrix[0:TILE, 512 * i : 512 * (i + 1)] for i in R4]
    top = {"y": (0,)}
    out0 = along("x", [(0, 3), (1, 2)], 0, top)
    sides = {"x": (0, 1)}
    a1 = send(pick(quarters[2], quarters[1]), out0 + along("y", [(0, 1)], 1, sides))
    a2 = send(pick(quarters[3], quarters[2]), out0 + along("y", [(0, 2)], 1, sides))
    a3 = send(quarters[3], along("y", [(0, 3)], 1, sides))
    qa = jnp.where(x < 2, quarters[0], a1)
    qb = jnp.where(x < 2, quarters[1], a2)
    s = jnp.where(y == 0, quarters[0], jnp.where(y == 1, a1, jnp.where(y == 2, a2, a3)))
    b1 = send(pick(qa, s), along("y", [(0, 1)], 0) + along("x", [(0, 1), (1, 0)], 1))
    b2 = send(pick(qb, s), along("y", [(0, 3)], 0) + along("x", [(0, 3), (1, 2)], 1))
    b3 = send(
        pick(jnp.where(y == 0, qa, b1), b2),
        along("y", [(0, 3), (1, 2)], 0) + along("x", [(3, 2), (2, 3)], 1),
    )
    b4 = send(jnp.where(y == 0, qb, b2), along("y", [(0, 1), (3, 2)], 0))
    qa = jnp.where(y == 0, qa, jnp.where(y == 1, b1, b3))
    qb = jnp.where(y == 0, qb, jnp.where(y == 3, b2, b4))
    p0 = jnp.where(x == 0, s, jnp.where(x == 1, b1, jnp.where(x == 2, b3, b2)))
    p1 = jnp.where(x == 0, b1, jnp.where(x == 1, s, jnp.where(x == 2, b2, b3)))
    both = jnp.stack([pick(qa, p0), pick(qb, p1)])
    pieces = [both]
    for k in (1, 2, 3):
        turn = [(i, (i + k) % 4) for i in R4]
        pieces.append(send(both, along("x", turn, 0) + along("y", turn, 1)))

    where = jnp.stack([row, col]).astype(jnp.int32)
    return update(where, matrix, v00, v10, v11, l00, l11, mine, other, pieces)


def solution(mesh):
    return jax.shard_map(
        shards,
        mesh=mesh,
        in_specs=(P("row", "col"),),
        out_specs=P("row", "col"),
        check_vma=False,
    )
```

```python
import functools

import jax
import jax.numpy as jnp
from jax import lax
from jax.experimental import pallas as pl
from jax.experimental.pallas import tpu as pltpu
from jax.sharding import PartitionSpec as P

TILE = 256
BLOCK = 128
F32 = jnp.float32
BF16 = jnp.bfloat16
HIGHEST = lax.Precision.HIGHEST


def device_id(y, x, z, c):
    return ((4 * y + x) * 4 + z) * 2 + c


def pairs(moves):
    return [(device_id(*a), device_id(*b)) for a, b in moves]


R4 = range(4)
R2 = range(2)


def send(value, moves):
    return lax.ppermute(value, ("row", "col"), pairs(moves))


def split3(x):
    hi = x.astype(BF16).astype(F32)
    rest = x - hi
    mid = rest.astype(BF16).astype(F32)
    return hi, mid, rest - mid


def stacked(x, left):
    hi, mid, lo = split3(x)
    parts = [hi, hi, mid, hi, lo, mid] if left else [hi, mid, hi, lo, hi, mid]
    return jnp.concatenate(parts, axis=0).astype(BF16)


def dot_tn(a, b, precision=None):
    return lax.dot_general(
        a, b, (((0,), (0,)), ((), ())), precision=precision, preferred_element_type=F32
    )


def spread(x):
    return jnp.broadcast_to(x, (8, BLOCK))


def factor_block(rows):
    groups, per = BLOCK // 8, 2
    width = 8 * per
    sub = lax.broadcasted_iota(jnp.int32, (8, BLOCK), 0)
    lane = lax.broadcasted_iota(jnp.int32, (8, BLOCK), 1)
    a = list(rows)
    w = [jnp.where(lane == sub + 8 * g, 1.0, 0.0).astype(F32) for g in range(groups)]
    upper, inverse = [], []
    for g in range(0, groups, per):
        r, v = a[g : g + per], w[g : g + per]
        cols = [[spread(x[:, 8 * g + i : 8 * g + i + 1]) for x in r] for i in range(width)]
        pivots = [None] * per
        for i in range(width):
            at, s = divmod(i, 8)
            p = spread(cols[i][at][s : s + 1, :])
            pivots[at] = p if s == 0 else jnp.where(sub == s, p, pivots[at])
            inverted = 1.0 / p
            row_r, row_v = spread(r[at][s : s + 1, :]), spread(v[at][s : s + 1, :])
            heads = [spread(cols[j][at][s : s + 1, :]) for j in range(i + 1, width)]
            for k in range(at, per):
                if k == at and s == 7:
                    continue
                m = cols[i][k] * inverted
                if k == at:
                    m = jnp.where(sub > s, m, 0.0)
                r[k] = r[k] - m * row_r
                v[k] = v[k] - m * row_v
                for j in range(i + 1, width):
                    cols[j][k] = cols[j][k] - m * heads[j - i - 1]
        for k in range(per):
            s = lax.rsqrt(pivots[k])
            s = s * (1.5 - 0.5 * pivots[k] * s * s)
            upper.append(jnp.where(lane >= sub + 8 * (g + k), r[k] * s, 0.0))
            inverse.append(v[k] * s)
        if g + per < groups:
            right = jnp.concatenate(upper[g:], axis=0)
            both = jnp.concatenate([right, jnp.concatenate(inverse[g:], axis=0)], axis=1)
            t = dot_tn(stacked(right, True), stacked(both, False))
            for h in range(g + per, groups):
                a[h] = a[h] - t[8 * h : 8 * h + 8, :BLOCK]
                w[h] = w[h] - t[8 * h : 8 * h + 8, BLOCK:]
    return jnp.concatenate(upper, axis=0), jnp.concatenate(inverse, axis=0)


def factor_tile(m, v_ref, l_ref):
    b = BLOCK
    u0, v0 = factor_block([m[8 * g : 8 * g + 8, 0:b] for g in range(b // 8)])
    u01 = jnp.dot(v0, m[0:b, b:], precision=HIGHEST, preferred_element_type=F32)
    m[b:, b:] = m[b:, b:] - dot_tn(u01, u01, HIGHEST)
    u1, v1 = factor_block([m[b + 8 * g : b + 8 * g + 8, b:] for g in range(b // 8)])
    w = dot_tn(u01, v0, HIGHEST)
    zeros = jnp.zeros((b, b), F32)
    v_ref[0:b, 0:b] = v0
    v_ref[0:b, b:] = zeros
    v_ref[b:, 0:b] = -jnp.dot(v1, w, precision=HIGHEST, preferred_element_type=F32)
    v_ref[b:, b:] = v1
    l_ref[0:b, 0:b] = u0.T
    l_ref[0:b, b:] = zeros
    l_ref[b:, 0:b] = u01.T
    l_ref[b:, b:] = u1.T


def first_kernel(d00, v00, l00, m):
    m[...] = d00[...]
    factor_tile(m, v00, l00)


def second_kernel(d10, d11, v00, v10, v11, l11, m):
    u01 = lax.dot_general(
        v00[...], d10[...], (((1,), (1,)), ((), ())), precision=HIGHEST, preferred_element_type=F32
    )
    m[...] = d11[...] - dot_tn(u01, u01, HIGHEST)
    factor_tile(m, v11, l11)
    w = dot_tn(u01, v00[...], HIGHEST)
    v10[...] = -jnp.dot(v11[...], w, precision=HIGHEST, preferred_element_type=F32)


def factor_call(kernel, sizes, args, scratch=()):
    vmem = pl.BlockSpec(memory_space=pltpu.VMEM)
    return pl.pallas_call(
        kernel,
        out_shape=[jax.ShapeDtypeStruct((n, n), F32) for n in sizes],
        in_specs=[vmem] * len(args),
        out_specs=[vmem] * len(sizes),
        scratch_shapes=list(scratch),
        compiler_params=pltpu.CompilerParams(vmem_limit_bytes=8 * 2**20),
        cost_estimate=pl.CostEstimate(
            flops=6 * 10**9, bytes_accessed=2**20, transcendentals=0
        ),
    )(*args)


def halves(x):
    hi = x.astype(BF16)
    return hi, (x - hi.astype(F32)).astype(BF16)


def dot3(a, b, dims):
    ah, al = a
    bh, bl = b
    d = (dims, ((), ()))
    out = lax.dot_general(ah, bh, d, preferred_element_type=F32)
    out = out + lax.dot_general(ah, bl, d, preferred_element_type=F32)
    return out + lax.dot_general(al, bh, d, preferred_element_type=F32)


NT = ((1,), (1,))
NN = ((1,), (0,))
CHUNK = 512


def update_kernel(shifts, solve, place, mat, v00_ref, v10_ref, v11_ref, l00, l11, *refs):
    if solve:
        mine, other, *pieces = refs[: 2 + len(shifts)]
        out, lph, lpl = refs[2 + len(shifts) : 5 + len(shifts)]
    else:
        lph, lpl, *pieces = refs[: 2 + len(shifts)]
        out = refs[3 + len(shifts)]
    m, o, lqh, lql, in_sem, out_sem = refs[-6:]
    row, col = place[0], place[1]
    zero_core = col % 2 == 0
    major = jnp.where(zero_core, row % 4, row // 4)
    rows = mat.shape[0]
    count = len(shifts)
    sources = [lax.rem(major + 4 - k, 4) for k in shifts]
    spans = [pl.ds(pl.multiple_of(i * CHUNK, CHUNK), CHUNK) for i in sources]
    loads = []
    for k in range(count):
        copy = pltpu.make_async_copy(mat.at[:, spans[k]], m.at[k], in_sem.at[k])
        copy.start()
        loads.append(copy)

    v00 = halves(v00_ref[...])
    v10 = halves(v10_ref[...])
    v11 = halves(v11_ref[...])

    for i in range(rows // TILE if solve else 0):
        at = pl.ds(i * TILE, TILE)
        a_mine, a_other = mine[at, :], other[at, :]
        a0 = halves(jnp.where(zero_core, a_mine, a_other))
        a1 = halves(jnp.where(zero_core, a_other, a_mine))
        lph[at, 0:TILE], lpl[at, 0:TILE] = halves(dot3(a0, v00, NT))
        lph[at, TILE:], lpl[at, TILE:] = halves(dot3(a0, v10, NT) + dot3(a1, v11, NT))

    stores = []
    for k in range(count):
        piece = pieces[k]
        slot = k
        d0 = halves(piece[0])
        d1 = halves(piece[1])
        lqh[0:TILE, :], lql[0:TILE, :] = halves(dot3(v00, d0, NN))
        lqh[TILE:, :], lql[TILE:, :] = halves(dot3(v10, d0, NN) + dot3(v11, d1, NN))
        loads[k].wait()
        for i in range(rows // TILE):
            r = pl.ds(i * TILE, TILE)
            o[slot, r, :] = m[k, r, :] - dot3(
                (lph[r, :], lpl[r, :]), (lqh[...], lql[...]), NN
            )

        @pl.when(row < 2)
        def _():
            o[slot, 0:TILE, :] = jnp.zeros((TILE, CHUNK), F32)

        @pl.when((sources[k] == 0) & (col < 2))
        def _():
            for j in range(2):
                side = pl.ds(j * TILE, TILE)

                @pl.when(col == j)
                def _():
                    o[slot, :, 0:TILE] = lph[:, side].astype(F32) + lpl[:, side].astype(F32)

            @pl.when((row == 0) & (col == 0))
            def _():
                o[slot, 0:TILE, 0:TILE] = l00[...]

            @pl.when((row == 0) & (col == 1))
            def _():
                o[slot, 0:TILE, 0:TILE] = jnp.zeros((TILE, TILE), F32)

            @pl.when((row == 1) & (col == 1))
            def _():
                o[slot, 0:TILE, 0:TILE] = l11[...]

        copy = pltpu.make_async_copy(o.at[slot], out.at[:, spans[k]], out_sem.at[k])
        copy.start()
        stores.append(copy)
    for copy in stores:
        copy.wait()


def update_call(shifts, place, mat, factors, pieces, rows_in=None, solved=None, out=None):
    rows, cols = mat.shape
    n = 2 * TILE
    solve = rows_in is not None
    count = len(shifts)
    hbm = pl.BlockSpec(memory_space=pl.ANY)
    vmem = pl.BlockSpec(memory_space=pltpu.VMEM)
    smem = pl.BlockSpec(memory_space=pltpu.SMEM)
    whole = jax.ShapeDtypeStruct((rows, cols), F32)
    half_rows = jax.ShapeDtypeStruct((rows, n), BF16)
    args = (place, mat, *factors, *(rows_in if solve else solved), *pieces)
    in_specs = [smem, hbm] + [vmem] * (len(args) - 2)
    if not solve:
        args += (out,)
        in_specs.append(hbm)
    return pl.pallas_call(
        functools.partial(update_kernel, shifts, solve),
        out_shape=[whole, half_rows, half_rows] if solve else whole,
        in_specs=in_specs,
        out_specs=[hbm, vmem, vmem] if solve else hbm,
        scratch_shapes=[
            pltpu.VMEM((count, rows, CHUNK), F32),
            pltpu.VMEM((count, rows, CHUNK), F32),
            pltpu.VMEM((n, CHUNK), BF16),
            pltpu.VMEM((n, CHUNK), BF16),
            pltpu.SemaphoreType.DMA((count,)),
            pltpu.SemaphoreType.DMA((count,)),
        ],
        input_output_aliases={} if solve else {len(args) - 1: 0},
        compiler_params=pltpu.CompilerParams(vmem_limit_bytes=26 * 2**20),
        cost_estimate=pl.CostEstimate(
            flops=3 * 10**9 * count, bytes_accessed=6 * 2**20 * count, transcendentals=0
        ),
    )(*args)


def along(axis, table, core, fixed=None):
    fixed = fixed or {}
    moves = []
    spans = [fixed.get(k, R4) for k in "yxz"]
    at = "yxz".index(axis)
    for a, b in table:
        spans[at] = (a,)
        for y in spans[0]:
            for x in spans[1]:
                for z in spans[2]:
                    dst = [y, x, z, core]
                    dst[at] = b
                    moves.append(((y, x, z, core), tuple(dst)))
    return moves


def swap_cores(value):
    return send(value, [((y, x, z, c), (y, x, z, 1 - c)) for y in R4 for x in R4 for z in R4 for c in R2])


def tied(values, *after):
    return lax.optimization_barrier((values, after))[0]


def shards(matrix):
    row = lax.axis_index("row")
    col = lax.axis_index("col")
    y, x = row // 4, row % 4
    z, c = col // 2, col % 2
    place = {"y": y, "x": x, "z": z, "c": c}
    zero_core = c == 0
    half = TILE // 2

    def pick(a, b):
        return jnp.where(zero_core, a, b)

    def columns(i):
        return lax.dynamic_slice(matrix, (0, i * CHUNK), (TILE, CHUNK))

    def among(index, *values):
        out = values[-1]
        for i in reversed(range(len(values) - 1)):
            out = jnp.where(index == i, values[i], out)
        return out

    tile = matrix[0:TILE, 0:TILE]
    strip = matrix[:, 0:TILE]

    first_stop = pick(1, 3)
    turns = (
        along("z", [(0, 1)], 0) + along("z", [(0, 3)], 1),
        along("z", [(0, 3), (1, 2)], 0) + along("z", [(0, 1), (3, 2)], 1),
    )
    spots = [((y0, x0, 0, c0), (y0, x0, k, c0)) for k in (2, 1, 3) for y0, x0, c0 in ((0, 0, 0), (0, 1, 0), (0, 1, 1))]
    t2, t1, t3 = [send(tile, spots[i : i + 3]) for i in (0, 3, 6)]
    tile = among(z, tile, t1, t2, t3)

    edge = {"y": (0,)}
    sides = {"x": (0, 1)}
    hops = (
        along("x", [(0, 1), (1, 0)], 0, edge) + along("y", [(0, 1)], 1, sides),
        along("x", [(0, 3), (1, 2)], 0, edge) + along("y", [(0, 2)], 1, sides),
        along("x", [(0, 2), (1, 3)], 0, edge) + along("y", [(0, 3)], 1, sides),
    )
    q0, *rest = [columns(i) for i in (
        pick(jnp.minimum(x, 1), 0),
        pick(1 - jnp.minimum(x, 1), 1),
        pick(jnp.where(x == 0, 3, 2), 2),
        pick(jnp.where(x == 0, 2, 3), 3),
    )]
    came = [send(q, moves) for q, moves in zip(rest, hops)]
    tiles = [send(tile, moves) for moves in hops]
    q0 = jnp.concatenate([q0, tile], axis=1)
    a1, a2, a3 = [jnp.concatenate(both, axis=1) for both in zip(came, tiles)]
    top = among(pick(x, y), q0, a1, pick(a3, a2), pick(a2, a3))
    low = among(pick(x, y), pick(a1, q0), pick(q0, a1), a2, a3)
    b1 = send(top, along("y", [(0, 1)], 0) + along("x", [(0, 1), (1, 0)], 1))
    b2 = send(low, along("y", [(0, 3)], 0) + along("x", [(0, 3), (1, 2)], 1))
    b3 = send(
        pick(jnp.where(y == 0, top, b1), b2),
        along("y", [(0, 3), (1, 2)], 0) + along("x", [(3, 2), (2, 3)], 1),
    )
    b4 = send(jnp.where(y == 0, low, b2), along("y", [(0, 1), (3, 2)], 0))
    first = among(pick(y, x), top, b1, b3, pick(b3, b2))
    second = among(pick(y, x), pick(low, b1), pick(b4, low), pick(b4, b2), pick(b2, b3))
    diagonal = jnp.stack([first[:, CHUNK:], second[:, CHUNK:]])
    both = jnp.stack([first[:, :CHUNK], second[:, :CHUNK]])
    diagonal_rest = swap_cores(diagonal)
    pieces = [both]
    for k in (1, 2, 3):
        turn = [(i, (i + k) % 4) for i in R4]
        pieces.append(send(both, along("x", turn, 0) + along("y", turn, 1)))
    d00 = pick(diagonal[0], diagonal_rest[0])
    d10 = pick(diagonal[1], diagonal_rest[1])
    d11 = pick(diagonal_rest[1], diagonal[1])
    scratch = [pltpu.VMEM((TILE, TILE), F32)]
    v00, l00 = factor_call(first_kernel, [TILE] * 2, (d00,), scratch)
    v10, v11, l11 = factor_call(second_kernel, [TILE] * 3, (d10, d11, v00), scratch)

    r1 = send(tied(strip, t2), turns[0])
    strip = jnp.where(z == first_stop, r1, strip)
    r2 = send(strip, turns[1])
    mine = jnp.where((z == 0) | (z == first_stop), strip, r2)
    other = swap_cores(mine)

    where = jnp.stack([row, col]).astype(jnp.int32)
    factors = (v00, v10, v11, l00, l11)
    out, high, rest = update_call((0,), where, matrix, factors, pieces[:1], rows_in=(mine, other))
    return update_call(
        (1, 3, 2), where, matrix, factors, (pieces[1], pieces[3], pieces[2]), solved=(high, rest), out=out
    )


def solution(mesh):
    return jax.shard_map(
        shards,
        mesh=mesh,
        in_specs=(P("row", "col"),),
        out_specs=P("row", "col"),
        check_vma=False,
    )
```

```python
import functools

import jax
import jax.numpy as jnp
from jax import lax
from jax.experimental import pallas as pl
from jax.experimental.pallas import tpu as pltpu
from jax.sharding import PartitionSpec as P

TILE = 256
BLOCK = 128
F32 = jnp.float32
BF16 = jnp.bfloat16
HIGHEST = lax.Precision.HIGHEST


def device_id(y, x, z, c):
    return ((4 * y + x) * 4 + z) * 2 + c


def pairs(moves):
    return [(device_id(*a), device_id(*b)) for a, b in moves]


R4 = range(4)
R2 = range(2)


def send(value, moves):
    return lax.ppermute(value, ("row", "col"), pairs(moves))


def split3(x):
    hi = x.astype(BF16).astype(F32)
    rest = x - hi
    mid = rest.astype(BF16).astype(F32)
    return hi, mid, rest - mid


def stacked(x, left):
    hi, mid, lo = split3(x)
    parts = [hi, hi, mid, hi, lo, mid] if left else [hi, mid, hi, lo, hi, mid]
    return jnp.concatenate(parts, axis=0).astype(BF16)


def dot_tn(a, b, precision=None):
    return lax.dot_general(
        a, b, (((0,), (0,)), ((), ())), precision=precision, preferred_element_type=F32
    )


def spread(x):
    return jnp.broadcast_to(x, (8, BLOCK))


def factor_block(rows):
    groups, per = BLOCK // 8, 2
    width = 8 * per
    sub = lax.broadcasted_iota(jnp.int32, (8, BLOCK), 0)
    lane = lax.broadcasted_iota(jnp.int32, (8, BLOCK), 1)
    a = list(rows)
    w = [jnp.where(lane == sub + 8 * g, 1.0, 0.0).astype(F32) for g in range(groups)]
    upper, inverse = [], []
    for g in range(0, groups, per):
        r, v = a[g : g + per], w[g : g + per]
        cols = [[spread(x[:, 8 * g + i : 8 * g + i + 1]) for x in r] for i in range(width)]
        pivots = [None] * per
        for i in range(width):
            at, s = divmod(i, 8)
            p = spread(cols[i][at][s : s + 1, :])
            pivots[at] = p if s == 0 else jnp.where(sub == s, p, pivots[at])
            inverted = 1.0 / p
            row_r, row_v = spread(r[at][s : s + 1, :]), spread(v[at][s : s + 1, :])
            heads = [spread(cols[j][at][s : s + 1, :]) for j in range(i + 1, width)]
            for k in range(at, per):
                if k == at and s == 7:
                    continue
                m = cols[i][k] * inverted
                if k == at:
                    m = jnp.where(sub > s, m, 0.0)
                r[k] = r[k] - m * row_r
                v[k] = v[k] - m * row_v
                for j in range(i + 1, width):
                    cols[j][k] = cols[j][k] - m * heads[j - i - 1]
        for k in range(per):
            s = lax.rsqrt(pivots[k])
            s = s * (1.5 - 0.5 * pivots[k] * s * s)
            upper.append(jnp.where(lane >= sub + 8 * (g + k), r[k] * s, 0.0))
            inverse.append(v[k] * s)
        if g + per < groups:
            right = jnp.concatenate(upper[g:], axis=0)
            both = jnp.concatenate([right, jnp.concatenate(inverse[g:], axis=0)], axis=1)
            t = dot_tn(stacked(right, True), stacked(both, False))
            for h in range(g + per, groups):
                a[h] = a[h] - t[8 * h : 8 * h + 8, :BLOCK]
                w[h] = w[h] - t[8 * h : 8 * h + 8, BLOCK:]
    return jnp.concatenate(upper, axis=0), jnp.concatenate(inverse, axis=0)


def factor_tile(m, v_ref, l_ref):
    b = BLOCK
    u0, v0 = factor_block([m[8 * g : 8 * g + 8, 0:b] for g in range(b // 8)])
    u01 = jnp.dot(v0, m[0:b, b:], precision=HIGHEST, preferred_element_type=F32)
    m[b:, b:] = m[b:, b:] - dot_tn(u01, u01, HIGHEST)
    u1, v1 = factor_block([m[b + 8 * g : b + 8 * g + 8, b:] for g in range(b // 8)])
    w = dot_tn(u01, v0, HIGHEST)
    zeros = jnp.zeros((b, b), F32)
    v_ref[0:b, 0:b] = v0
    v_ref[0:b, b:] = zeros
    v_ref[b:, 0:b] = -jnp.dot(v1, w, precision=HIGHEST, preferred_element_type=F32)
    v_ref[b:, b:] = v1
    l_ref[0:b, 0:b] = u0.T
    l_ref[0:b, b:] = zeros
    l_ref[b:, 0:b] = u01.T
    l_ref[b:, b:] = u1.T


def first_kernel(d00, v00, l00, m):
    m[...] = d00[...]
    factor_tile(m, v00, l00)


def second_kernel(d10, d11, v00, v10, v11, l11, m):
    u01 = lax.dot_general(
        v00[...], d10[...], (((1,), (1,)), ((), ())), precision=HIGHEST, preferred_element_type=F32
    )
    m[...] = d11[...] - dot_tn(u01, u01, HIGHEST)
    factor_tile(m, v11, l11)
    w = dot_tn(u01, v00[...], HIGHEST)
    v10[...] = -jnp.dot(v11[...], w, precision=HIGHEST, preferred_element_type=F32)


def factor_call(kernel, sizes, args, scratch=()):
    vmem = pl.BlockSpec(memory_space=pltpu.VMEM)
    return pl.pallas_call(
        kernel,
        out_shape=[jax.ShapeDtypeStruct((n, n), F32) for n in sizes],
        in_specs=[vmem] * len(args),
        out_specs=[vmem] * len(sizes),
        scratch_shapes=list(scratch),
        compiler_params=pltpu.CompilerParams(vmem_limit_bytes=8 * 2**20),
        cost_estimate=pl.CostEstimate(
            flops=6 * 10**9, bytes_accessed=2**20, transcendentals=0
        ),
    )(*args)


def halves(x):
    hi = x.astype(BF16)
    return hi, (x - hi.astype(F32)).astype(BF16)


def dot3(a, b, dims):
    ah, al = a
    bh, bl = b
    d = (dims, ((), ()))
    out = lax.dot_general(ah, bh, d, preferred_element_type=F32)
    out = out + lax.dot_general(ah, bl, d, preferred_element_type=F32)
    return out + lax.dot_general(al, bh, d, preferred_element_type=F32)


NT = ((1,), (1,))
NN = ((1,), (0,))
CHUNK = 512


def update_kernel(shifts, solve, place, mat, v00_ref, v10_ref, v11_ref, l00, l11, *refs):
    if solve:
        mine, other, *pieces = refs[: 2 + len(shifts)]
        out, lph, lpl = refs[2 + len(shifts) : 5 + len(shifts)]
    else:
        lph, lpl, *pieces = refs[: 2 + len(shifts)]
        out = refs[3 + len(shifts)]
    m, o, lqh, lql, in_sem, out_sem = refs[-6:]
    row, col = place[0], place[1]
    zero_core = col % 2 == 0
    major = jnp.where(zero_core, row % 4, row // 4)
    rows = mat.shape[0]
    count = len(shifts)
    sources = [lax.rem(major + 4 - k, 4) for k in shifts]
    spans = [pl.ds(pl.multiple_of(i * CHUNK, CHUNK), CHUNK) for i in sources]
    loads = []
    for k in range(count):
        copy = pltpu.make_async_copy(mat.at[:, spans[k]], m.at[k], in_sem.at[k])
        copy.start()
        loads.append(copy)

    v00 = halves(v00_ref[...])
    v10 = halves(v10_ref[...])
    v11 = halves(v11_ref[...])

    for i in range(rows // TILE if solve else 0):
        at = pl.ds(i * TILE, TILE)
        a_mine, a_other = mine[at, :], other[at, :]
        a0 = halves(jnp.where(zero_core, a_mine, a_other))
        a1 = halves(jnp.where(zero_core, a_other, a_mine))
        lph[at, 0:TILE], lpl[at, 0:TILE] = halves(dot3(a0, v00, NT))
        lph[at, TILE:], lpl[at, TILE:] = halves(dot3(a0, v10, NT) + dot3(a1, v11, NT))

    stores = []
    for k in range(count):
        piece = pieces[k]
        slot = k
        d0 = halves(piece[0])
        d1 = halves(piece[1])
        lqh[0:TILE, :], lql[0:TILE, :] = halves(dot3(v00, d0, NN))
        lqh[TILE:, :], lql[TILE:, :] = halves(dot3(v10, d0, NN) + dot3(v11, d1, NN))
        loads[k].wait()
        for i in range(rows // TILE):
            r = pl.ds(i * TILE, TILE)
            o[slot, r, :] = m[k, r, :] - dot3(
                (lph[r, :], lpl[r, :]), (lqh[...], lql[...]), NN
            )

        @pl.when(row < 2)
        def _():
            o[slot, 0:TILE, :] = jnp.zeros((TILE, CHUNK), F32)

        @pl.when((sources[k] == 0) & (col < 2))
        def _():
            for j in range(2):
                side = pl.ds(j * TILE, TILE)

                @pl.when(col == j)
                def _():
                    o[slot, :, 0:TILE] = lph[:, side].astype(F32) + lpl[:, side].astype(F32)

            @pl.when((row == 0) & (col == 0))
            def _():
                o[slot, 0:TILE, 0:TILE] = l00[...]

            @pl.when((row == 0) & (col == 1))
            def _():
                o[slot, 0:TILE, 0:TILE] = jnp.zeros((TILE, TILE), F32)

            @pl.when((row == 1) & (col == 1))
            def _():
                o[slot, 0:TILE, 0:TILE] = l11[...]

        copy = pltpu.make_async_copy(o.at[slot], out.at[:, spans[k]], out_sem.at[k])
        copy.start()
        stores.append(copy)
    for copy in stores:
        copy.wait()


def update_call(shifts, place, mat, factors, pieces, rows_in=None, solved=None, out=None):
    rows, cols = mat.shape
    n = 2 * TILE
    solve = rows_in is not None
    count = len(shifts)
    hbm = pl.BlockSpec(memory_space=pl.ANY)
    vmem = pl.BlockSpec(memory_space=pltpu.VMEM)
    smem = pl.BlockSpec(memory_space=pltpu.SMEM)
    whole = jax.ShapeDtypeStruct((rows, cols), F32)
    half_rows = jax.ShapeDtypeStruct((rows, n), BF16)
    args = (place, mat, *factors, *(rows_in if solve else solved), *pieces)
    in_specs = [smem, hbm] + [vmem] * (len(args) - 2)
    if not solve:
        args += (out,)
        in_specs.append(hbm)
    return pl.pallas_call(
        functools.partial(update_kernel, shifts, solve),
        out_shape=[whole, half_rows, half_rows] if solve else whole,
        in_specs=in_specs,
        out_specs=[hbm, vmem, vmem] if solve else hbm,
        scratch_shapes=[
            pltpu.VMEM((count, rows, CHUNK), F32),
            pltpu.VMEM((count, rows, CHUNK), F32),
            pltpu.VMEM((n, CHUNK), BF16),
            pltpu.VMEM((n, CHUNK), BF16),
            pltpu.SemaphoreType.DMA((count,)),
            pltpu.SemaphoreType.DMA((count,)),
        ],
        input_output_aliases={} if solve else {len(args) - 1: 0},
        compiler_params=pltpu.CompilerParams(vmem_limit_bytes=26 * 2**20),
        cost_estimate=pl.CostEstimate(
            flops=3 * 10**9 * count, bytes_accessed=6 * 2**20 * count, transcendentals=0
        ),
    )(*args)


def along(axis, table, core, fixed=None):
    fixed = fixed or {}
    moves = []
    spans = [fixed.get(k, R4) for k in "yxz"]
    at = "yxz".index(axis)
    for a, b in table:
        spans[at] = (a,)
        for y in spans[0]:
            for x in spans[1]:
                for z in spans[2]:
                    dst = [y, x, z, core]
                    dst[at] = b
                    moves.append(((y, x, z, core), tuple(dst)))
    return moves


def swap_cores(value):
    return send(value, [((y, x, z, c), (y, x, z, 1 - c)) for y in R4 for x in R4 for z in R4 for c in R2])


def tied(values, *after):
    return lax.optimization_barrier((values, after))[0]


def shards(matrix):
    row = lax.axis_index("row")
    col = lax.axis_index("col")
    y, x = row // 4, row % 4
    z, c = col // 2, col % 2
    place = {"y": y, "x": x, "z": z, "c": c}
    zero_core = c == 0
    half = TILE // 2

    def pick(a, b):
        return jnp.where(zero_core, a, b)

    def columns(i):
        return lax.dynamic_slice(matrix, (0, i * CHUNK), (TILE, CHUNK))

    def among(index, *values):
        out = values[-1]
        for i in reversed(range(len(values) - 1)):
            out = jnp.where(index == i, values[i], out)
        return out

    tile = matrix[0:TILE, 0:TILE]
    strip = matrix[:, 0:TILE]

    first_stop = pick(1, 3)
    turns = (
        along("z", [(0, 1)], 0) + along("z", [(0, 3)], 1),
        along("z", [(0, 3), (1, 2)], 0) + along("z", [(0, 1), (3, 2)], 1),
    )
    spots = [((y0, x0, 0, c0), (y0, x0, k, c0)) for k in (2, 1, 3) for y0, x0, c0 in ((0, 0, 0), (0, 1, 0), (0, 1, 1))]
    q0, *rest = [columns(i) for i in (
        pick(jnp.minimum(x, 1), 0),
        pick(1 - jnp.minimum(x, 1), 1),
        pick(jnp.where(x == 0, 3, 2), 2),
        pick(jnp.where(x == 0, 2, 3), 3),
    )]
    tile = tied(tile, q0, *rest)
    t2, t1, t3 = [send(tile, spots[i : i + 3]) for i in (0, 3, 6)]
    tile = among(z, tile, t1, t2, t3)

    edge = {"y": (0,)}
    sides = {"x": (0, 1)}
    hops = (
        along("x", [(0, 1), (1, 0)], 0, edge) + along("y", [(0, 1)], 1, sides),
        along("x", [(0, 3), (1, 2)], 0, edge) + along("y", [(0, 2)], 1, sides),
        along("x", [(0, 2), (1, 3)], 0, edge) + along("y", [(0, 3)], 1, sides),
    )
    came = [send(q, moves) for q, moves in zip(rest, hops)]
    tiles = [send(tile, moves) for moves in hops]
    q0 = jnp.concatenate([q0, tile], axis=1)
    a1, a2, a3 = [jnp.concatenate(both, axis=1) for both in zip(came, tiles)]
    top = among(pick(x, y), q0, a1, pick(a3, a2), pick(a2, a3))
    low = among(pick(x, y), pick(a1, q0), pick(q0, a1), a2, a3)
    b1 = send(top, along("y", [(0, 1)], 0) + along("x", [(0, 1), (1, 0)], 1))
    b2 = send(low, along("y", [(0, 3)], 0) + along("x", [(0, 3), (1, 2)], 1))
    b3 = send(top, along("y", [(0, 3)], 0))
    b4 = send(low, along("y", [(0, 1)], 0))
    b5 = send(pick(b1, b2), along("y", [(1, 2)], 0) + along("x", [(3, 2), (2, 3)], 1))
    b6 = send(b2, along("y", [(3, 2)], 0))
    first = among(pick(y, x), top, b1, b5, pick(b3, b2))
    second = among(pick(y, x), pick(low, b1), pick(b4, low), pick(b6, b2), pick(b2, b5))
    diagonal = jnp.stack([first[:, CHUNK:], second[:, CHUNK:]])
    both = jnp.stack([first[:, :CHUNK], second[:, :CHUNK]])
    diagonal_rest = swap_cores(diagonal)
    pieces = [both]
    for k in (1, 2, 3):
        turn = [(i, (i + k) % 4) for i in R4]
        pieces.append(send(both, along("x", turn, 0) + along("y", turn, 1)))
    d00 = pick(diagonal[0], diagonal_rest[0])
    d10 = pick(diagonal[1], diagonal_rest[1])
    d11 = pick(diagonal_rest[1], diagonal[1])
    scratch = [pltpu.VMEM((TILE, TILE), F32)]
    v00, l00 = factor_call(first_kernel, [TILE] * 2, (d00,), scratch)
    v10, v11, l11 = factor_call(second_kernel, [TILE] * 3, (d10, d11, v00), scratch)

    r1 = send(tied(strip, t2), turns[0])
    strip = jnp.where(z == first_stop, r1, strip)
    r2 = send(strip, turns[1])
    mine = jnp.where((z == 0) | (z == first_stop), strip, r2)
    other = swap_cores(mine)

    where = jnp.stack([row, col]).astype(jnp.int32)
    factors = (v00, v10, v11, l00, l11)
    out, high, rest = update_call((0,), where, matrix, factors, pieces[:1], rows_in=(mine, other))
    return update_call(
        (1, 3, 2), where, matrix, factors, (pieces[1], pieces[3], pieces[2]), solved=(high, rest), out=out
    )


def solution(mesh):
    return jax.shard_map(
        shards,
        mesh=mesh,
        in_specs=(P("row", "col"),),
        out_specs=P("row", "col"),
        check_vma=False,
    )
```

```python
import functools

import jax
import jax.numpy as jnp
from jax import lax
from jax.experimental import pallas as pl
from jax.experimental.pallas import tpu as pltpu
from jax.sharding import PartitionSpec as P

TILE = 256
BLOCK = 128
F32 = jnp.float32
BF16 = jnp.bfloat16
HIGHEST = lax.Precision.HIGHEST


def device_id(y, x, z, c):
    return ((4 * y + x) * 4 + z) * 2 + c


def pairs(moves):
    return [(device_id(*a), device_id(*b)) for a, b in moves]


R4 = range(4)
R2 = range(2)


def send(value, moves):
    return lax.ppermute(value, ("row", "col"), pairs(moves))


def split3(x):
    hi = x.astype(BF16).astype(F32)
    rest = x - hi
    mid = rest.astype(BF16).astype(F32)
    return hi, mid, rest - mid


def stacked(x, left):
    hi, mid, lo = split3(x)
    parts = [hi, hi, mid, hi, lo, mid] if left else [hi, mid, hi, lo, hi, mid]
    return jnp.concatenate(parts, axis=0).astype(BF16)


def dot_tn(a, b, precision=None):
    return lax.dot_general(
        a, b, (((0,), (0,)), ((), ())), precision=precision, preferred_element_type=F32
    )


def spread(x):
    return jnp.broadcast_to(x, (8, BLOCK))


def factor_block(rows):
    groups, per = BLOCK // 8, 2
    width = 8 * per
    sub = lax.broadcasted_iota(jnp.int32, (8, BLOCK), 0)
    lane = lax.broadcasted_iota(jnp.int32, (8, BLOCK), 1)
    a = list(rows)
    w = [jnp.where(lane == sub + 8 * g, 1.0, 0.0).astype(F32) for g in range(groups)]
    upper, inverse = [], []
    for g in range(0, groups, per):
        r, v = a[g : g + per], w[g : g + per]
        cols = [[spread(x[:, 8 * g + i : 8 * g + i + 1]) for x in r] for i in range(width)]
        pivots = [None] * per
        for i in range(width):
            at, s = divmod(i, 8)
            p = spread(cols[i][at][s : s + 1, :])
            pivots[at] = p if s == 0 else jnp.where(sub == s, p, pivots[at])
            inverted = 1.0 / p
            row_r, row_v = spread(r[at][s : s + 1, :]), spread(v[at][s : s + 1, :])
            heads = [spread(cols[j][at][s : s + 1, :]) for j in range(i + 1, width)]
            for k in range(at, per):
                if k == at and s == 7:
                    continue
                m = cols[i][k] * inverted
                if k == at:
                    m = jnp.where(sub > s, m, 0.0)
                r[k] = r[k] - m * row_r
                v[k] = v[k] - m * row_v
                for j in range(i + 1, width):
                    cols[j][k] = cols[j][k] - m * heads[j - i - 1]
        for k in range(per):
            s = lax.rsqrt(pivots[k])
            s = s * (1.5 - 0.5 * pivots[k] * s * s)
            upper.append(jnp.where(lane >= sub + 8 * (g + k), r[k] * s, 0.0))
            inverse.append(v[k] * s)
        if g + per < groups:
            right = jnp.concatenate(upper[g:], axis=0)
            both = jnp.concatenate([right, jnp.concatenate(inverse[g:], axis=0)], axis=1)
            t = dot_tn(stacked(right, True), stacked(both, False))
            for h in range(g + per, groups):
                a[h] = a[h] - t[8 * h : 8 * h + 8, :BLOCK]
                w[h] = w[h] - t[8 * h : 8 * h + 8, BLOCK:]
    return jnp.concatenate(upper, axis=0), jnp.concatenate(inverse, axis=0)


def factor_tile(m, v_ref, l_ref):
    b = BLOCK
    u0, v0 = factor_block([m[8 * g : 8 * g + 8, 0:b] for g in range(b // 8)])
    u01 = jnp.dot(v0, m[0:b, b:], precision=HIGHEST, preferred_element_type=F32)
    m[b:, b:] = m[b:, b:] - dot_tn(u01, u01, HIGHEST)
    u1, v1 = factor_block([m[b + 8 * g : b + 8 * g + 8, b:] for g in range(b // 8)])
    w = dot3(halves(u01), halves(v0), TN)
    zeros = jnp.zeros((b, b), F32)
    v_ref[0:b, 0:b] = v0
    v_ref[0:b, b:] = zeros
    v_ref[b:, 0:b] = -dot3(halves(v1), halves(w), NN)
    v_ref[b:, b:] = v1
    l_ref[0:b, 0:b] = u0.T
    l_ref[0:b, b:] = zeros
    l_ref[b:, 0:b] = u01.T
    l_ref[b:, b:] = u1.T


def first_kernel(d00, v00, l00, m):
    m[...] = d00[...]
    factor_tile(m, v00, l00)


def second_kernel(d10, d11, v00, v10, v11, l11, m):
    u01 = lax.dot_general(
        v00[...], d10[...], (((1,), (1,)), ((), ())), precision=HIGHEST, preferred_element_type=F32
    )
    m[...] = d11[...] - dot_tn(u01, u01, HIGHEST)
    factor_tile(m, v11, l11)
    w = dot3(halves(u01), halves(v00[...]), TN)
    v10[...] = -dot3(halves(v11[...]), halves(w), NN)


def factor_call(kernel, sizes, args, scratch=()):
    vmem = pl.BlockSpec(memory_space=pltpu.VMEM)
    return pl.pallas_call(
        kernel,
        out_shape=[jax.ShapeDtypeStruct((n, n), F32) for n in sizes],
        in_specs=[vmem] * len(args),
        out_specs=[vmem] * len(sizes),
        scratch_shapes=list(scratch),
        compiler_params=pltpu.CompilerParams(vmem_limit_bytes=8 * 2**20),
        cost_estimate=pl.CostEstimate(
            flops=6 * 10**9, bytes_accessed=2**20, transcendentals=0
        ),
    )(*args)


def halves(x):
    hi = x.astype(BF16)
    return hi, (x - hi.astype(F32)).astype(BF16)


def dot3(a, b, dims):
    ah, al = a
    bh, bl = b
    d = (dims, ((), ()))
    out = lax.dot_general(ah, bh, d, preferred_element_type=F32)
    out = out + lax.dot_general(ah, bl, d, preferred_element_type=F32)
    return out + lax.dot_general(al, bh, d, preferred_element_type=F32)


TN = ((0,), (0,))
NT = ((1,), (1,))
NN = ((1,), (0,))
CHUNK = 512


def update_kernel(shifts, solve, place, mat, v00_ref, v10_ref, v11_ref, l00, l11, *refs):
    if solve:
        mine, other, *pieces = refs[: 2 + len(shifts)]
        out, lph, lpl = refs[2 + len(shifts) : 5 + len(shifts)]
    else:
        lph, lpl, *pieces = refs[: 2 + len(shifts)]
        out = refs[3 + len(shifts)]
    m, o, lqh, lql, in_sem, out_sem = refs[-6:]
    row, col = place[0], place[1]
    zero_core = col % 2 == 0
    major = jnp.where(zero_core, row % 4, row // 4)
    rows = mat.shape[0]
    count = len(shifts)
    sources = [lax.rem(major + 4 - k, 4) for k in shifts]
    spans = [pl.ds(pl.multiple_of(i * CHUNK, CHUNK), CHUNK) for i in sources]
    loads = []
    for k in range(count):
        copy = pltpu.make_async_copy(mat.at[:, spans[k]], m.at[k], in_sem.at[k])
        copy.start()
        loads.append(copy)

    v00 = halves(v00_ref[...])
    v10 = halves(v10_ref[...])
    v11 = halves(v11_ref[...])

    for i in range(rows // TILE if solve else 0):
        at = pl.ds(i * TILE, TILE)
        a_mine, a_other = mine[at, :], other[at, :]
        a0 = halves(jnp.where(zero_core, a_mine, a_other))
        a1 = halves(jnp.where(zero_core, a_other, a_mine))
        lph[at, 0:TILE], lpl[at, 0:TILE] = halves(dot3(a0, v00, NT))
        lph[at, TILE:], lpl[at, TILE:] = halves(dot3(a0, v10, NT) + dot3(a1, v11, NT))

    stores = []
    for k in range(count):
        piece = pieces[k]
        slot = k
        d0 = halves(piece[0])
        d1 = halves(piece[1])
        lqh[0:TILE, :], lql[0:TILE, :] = halves(dot3(v00, d0, NN))
        lqh[TILE:, :], lql[TILE:, :] = halves(dot3(v10, d0, NN) + dot3(v11, d1, NN))
        loads[k].wait()
        for i in range(rows // TILE):
            r = pl.ds(i * TILE, TILE)
            o[slot, r, :] = m[k, r, :] - dot3(
                (lph[r, :], lpl[r, :]), (lqh[...], lql[...]), NN
            )

        @pl.when(row < 2)
        def _():
            o[slot, 0:TILE, :] = jnp.zeros((TILE, CHUNK), F32)

        @pl.when((sources[k] == 0) & (col < 2))
        def _():
            for j in range(2):
                side = pl.ds(j * TILE, TILE)

                @pl.when(col == j)
                def _():
                    o[slot, :, 0:TILE] = lph[:, side].astype(F32) + lpl[:, side].astype(F32)

            @pl.when((row == 0) & (col == 0))
            def _():
                o[slot, 0:TILE, 0:TILE] = l00[...]

            @pl.when((row == 0) & (col == 1))
            def _():
                o[slot, 0:TILE, 0:TILE] = jnp.zeros((TILE, TILE), F32)

            @pl.when((row == 1) & (col == 1))
            def _():
                o[slot, 0:TILE, 0:TILE] = l11[...]

        copy = pltpu.make_async_copy(o.at[slot], out.at[:, spans[k]], out_sem.at[k])
        copy.start()
        stores.append(copy)
    for copy in stores:
        copy.wait()


def update_call(shifts, place, mat, factors, pieces, rows_in=None, solved=None, out=None):
    rows, cols = mat.shape
    n = 2 * TILE
    solve = rows_in is not None
    count = len(shifts)
    hbm = pl.BlockSpec(memory_space=pl.ANY)
    vmem = pl.BlockSpec(memory_space=pltpu.VMEM)
    smem = pl.BlockSpec(memory_space=pltpu.SMEM)
    whole = jax.ShapeDtypeStruct((rows, cols), F32)
    half_rows = jax.ShapeDtypeStruct((rows, n), BF16)
    args = (place, mat, *factors, *(rows_in if solve else solved), *pieces)
    in_specs = [smem, hbm] + [vmem] * (len(args) - 2)
    if not solve:
        args += (out,)
        in_specs.append(hbm)
    return pl.pallas_call(
        functools.partial(update_kernel, shifts, solve),
        out_shape=[whole, half_rows, half_rows] if solve else whole,
        in_specs=in_specs,
        out_specs=[hbm, vmem, vmem] if solve else hbm,
        scratch_shapes=[
            pltpu.VMEM((count, rows, CHUNK), F32),
            pltpu.VMEM((count, rows, CHUNK), F32),
            pltpu.VMEM((n, CHUNK), BF16),
            pltpu.VMEM((n, CHUNK), BF16),
            pltpu.SemaphoreType.DMA((count,)),
            pltpu.SemaphoreType.DMA((count,)),
        ],
        input_output_aliases={} if solve else {len(args) - 1: 0},
        compiler_params=pltpu.CompilerParams(vmem_limit_bytes=26 * 2**20),
        cost_estimate=pl.CostEstimate(
            flops=3 * 10**9 * count, bytes_accessed=6 * 2**20 * count, transcendentals=0
        ),
    )(*args)


def along(axis, table, core, fixed=None):
    fixed = fixed or {}
    moves = []
    spans = [fixed.get(k, R4) for k in "yxz"]
    at = "yxz".index(axis)
    for a, b in table:
        spans[at] = (a,)
        for y in spans[0]:
            for x in spans[1]:
                for z in spans[2]:
                    dst = [y, x, z, core]
                    dst[at] = b
                    moves.append(((y, x, z, core), tuple(dst)))
    return moves


def swap_cores(value):
    return send(value, [((y, x, z, c), (y, x, z, 1 - c)) for y in R4 for x in R4 for z in R4 for c in R2])


def tied(values, *after):
    return lax.optimization_barrier((values, after))[0]


def shards(matrix):
    row = lax.axis_index("row")
    col = lax.axis_index("col")
    y, x = row // 4, row % 4
    z, c = col // 2, col % 2
    place = {"y": y, "x": x, "z": z, "c": c}
    zero_core = c == 0
    half = TILE // 2

    def pick(a, b):
        return jnp.where(zero_core, a, b)

    def columns(i):
        return lax.dynamic_slice(matrix, (0, i * CHUNK), (TILE, CHUNK))

    def among(index, *values):
        out = values[-1]
        for i in reversed(range(len(values) - 1)):
            out = jnp.where(index == i, values[i], out)
        return out

    tile = matrix[0:TILE, 0:TILE]
    strip = matrix[:, 0:TILE]

    first_stop = pick(1, 3)
    turns = (
        along("z", [(0, 1)], 0) + along("z", [(0, 3)], 1),
        along("z", [(0, 3), (1, 2)], 0) + along("z", [(0, 1), (3, 2)], 1),
    )
    spots = [((y0, x0, 0, c0), (y0, x0, k, c0)) for k in (3, 2, 1) for y0, x0, c0 in ((0, 0, 0), (0, 1, 0), (0, 1, 1))]
    q0, *rest = [columns(i) for i in (
        pick(jnp.minimum(x, 1), 0),
        pick(1 - jnp.minimum(x, 1), 1),
        pick(jnp.where(x == 0, 3, 2), 2),
        pick(jnp.where(x == 0, 2, 3), 3),
    )]
    tile = tied(tile, q0, *rest)
    t3, t2, t1 = [send(tile, spots[i : i + 3]) for i in (0, 3, 6)]
    tile = among(z, tile, t1, t2, t3)

    edge = {"y": (0,)}
    sides = {"x": (0, 1)}
    hops = (
        along("x", [(0, 1), (1, 0)], 0, edge) + along("y", [(0, 1)], 1, sides),
        along("x", [(0, 3), (1, 2)], 0, edge) + along("y", [(0, 2)], 1, sides),
        along("x", [(0, 2), (1, 3)], 0, edge) + along("y", [(0, 3)], 1, sides),
    )
    came = [send(q, moves) for q, moves in zip(rest, hops)]
    tiles = [send(tile, moves) for moves in hops]
    q0 = jnp.concatenate([q0, tile], axis=1)
    a1, a2, a3 = [jnp.concatenate(both, axis=1) for both in zip(came, tiles)]
    top = among(pick(x, y), q0, a1, pick(a3, a2), pick(a2, a3))
    low = among(pick(x, y), pick(a1, q0), pick(q0, a1), a2, a3)
    b1 = send(top, along("y", [(0, 1)], 0) + along("x", [(0, 1), (1, 0)], 1))
    b2 = send(low, along("y", [(0, 3)], 0) + along("x", [(0, 3), (1, 2)], 1))
    b3 = send(top, along("y", [(0, 3)], 0))
    b4 = send(low, along("y", [(0, 1)], 0))
    b5 = send(pick(b1, b2), along("y", [(1, 2)], 0) + along("x", [(3, 2), (2, 3)], 1))
    b6 = send(b2, along("y", [(3, 2)], 0))
    first = among(pick(y, x), top, b1, b5, pick(b3, b2))
    second = among(pick(y, x), pick(low, b1), pick(b4, low), pick(b6, b2), pick(b2, b5))
    diagonal = jnp.stack([first[:, CHUNK:], second[:, CHUNK:]])
    both = jnp.stack([first[:, :CHUNK], second[:, :CHUNK]])
    diagonal_rest = swap_cores(diagonal)
    pieces = [both]
    for k in (1, 2, 3):
        turn = [(i, (i + k) % 4) for i in R4]
        pieces.append(send(both, along("x", turn, 0) + along("y", turn, 1)))
    d00 = pick(diagonal[0], diagonal_rest[0])
    d10 = pick(diagonal[1], diagonal_rest[1])
    d11 = pick(diagonal_rest[1], diagonal[1])
    scratch = [pltpu.VMEM((TILE, TILE), F32)]
    v00, l00 = factor_call(first_kernel, [TILE] * 2, (d00,), scratch)
    v10, v11, l11 = factor_call(second_kernel, [TILE] * 3, (d10, d11, v00), scratch)

    r1 = send(tied(strip, t1), turns[0])
    strip = jnp.where(z == first_stop, r1, strip)
    r2 = send(strip, turns[1])
    mine = jnp.where((z == 0) | (z == first_stop), strip, r2)
    other = swap_cores(mine)

    where = jnp.stack([row, col]).astype(jnp.int32)
    factors = (v00, v10, v11, l00, l11)
    out, high, rest = update_call((0,), where, matrix, factors, pieces[:1], rows_in=(mine, other))
    return update_call(
        (1, 3, 2), where, matrix, factors, (pieces[1], pieces[3], pieces[2]), solved=(high, rest), out=out
    )


def solution(mesh):
    return jax.shard_map(
        shards,
        mesh=mesh,
        in_specs=(P("row", "col"),),
        out_specs=P("row", "col"),
        check_vma=False,
    )
```
